32 devices in a mesh: rep: 16 (over z, x, core), shard: 2 (over y).
Axes of the slice: x: 2, y: 2, z: 4, core: 2. Of those that a mesh axis runs over, the one named last changes fastest.
Arguments:
- layer_input: bfloat16 [32768, 576], P(('rep', 'shard')), may hold values from -6 to 6
- seq_lengths: int32 [128], P(('rep', 'shard')), may hold values from 0 to 1024, as said below
- out_cotangent: bfloat16 [32768, 576], P(('rep', 'shard')), may hold values from -6 to 6
- attn_gain: bfloat16 [576], P('shard'), may hold values from 0.099609375 to 1.8984375
- w_query: bfloat16 [576, 576], P('shard'), may hold values from -0.25 to 0.25
- w_key: bfloat16 [576, 192], P('shard'), may hold values from -0.25 to 0.25
- w_value: bfloat16 [576, 192], P('shard'), may hold values from -0.25 to 0.25
- w_out: bfloat16 [576, 576], P('shard'), may hold values from -1.5 to 1.5
- mlp_gain: bfloat16 [576], P('shard'), may hold values from 0.099609375 to 1.8984375
- w_gate: bfloat16 [576, 1536], P('shard'), may hold values from -0.25 to 0.25
- w_up: bfloat16 [576, 1536], P('shard'), may hold values from -0.25 to 0.25
- w_down: bfloat16 [1536, 576], P('shard'), may hold values from -0.15625 to 0.15625
Outputs:
- layer_output: bfloat16 [32768, 576], P(('rep', 'shard'))
- input_grad: bfloat16 [32768, 576], P(('rep', 'shard'))
- attn_gain_grad: float32 [576], P('shard')
- w_query_grad: float32 [576, 576], P('shard')
- w_key_grad: float32 [576, 192], P('shard')
- w_value_grad: float32 [576, 192], P('shard')
- w_out_grad: float32 [576, 576], P('shard')
- mlp_gain_grad: float32 [576], P('shard')
- w_gate_grad: float32 [576, 1536], P('shard')
- w_up_grad: float32 [576, 1536], P('shard')
- w_down_grad: float32 [1536, 576], P('shard')
The draws below stay inside these ranges and needn't reach their ends.
Inputs may be any that keep to these rules, and one draw needn't show every extreme that they name: `seq_lengths`: each run of 4 entries belongs to one device. A length of 0 is an empty slot. On every device the sum over its slots of ceil(length / 128) is at most 8, and at least 4. Some device holds one sequence of exactly 1024 tokens.
All inputs are finite; a program needn't handle non-finite values.
Results may differ from the reference program's by a relative error of at most 0.02.
Values may be sent and summed in bfloat16 or wider, within the bound.
A program may use at most 128 MiB of HBM per device.

```python
import math
import jax
import jax.numpy as jnp
from jax import lax

HEADS = 9
KV_HEADS = 3
HEAD_DIM = 64
FF = 1536
D = 576
KV = 192
TOKENS_PER_SHARD = 1024
SEQS_DEV = 4
PAD_BLOCK = 128
TOKENS = 32768
N_REP = 16
N_SHARD = 2


def draw_seq_lengths(key, part):
    key = jax.random.fold_in(key, 11)
    device_count = N_REP * N_SHARD
    block_total = TOKENS_PER_SHARD // PAD_BLOCK
    key_used, key_cuts, key_tail, key_pick = jax.random.split(key, 4)
    used_blocks = jax.random.randint(key_used, (device_count, 1), SEQS_DEV, block_total + 1)
    cut_points = jax.random.randint(key_cuts, (device_count, SEQS_DEV - 1), 0, block_total + 1)
    cut_points = jnp.sort(jnp.minimum(cut_points, used_blocks), axis=1)
    edges = jnp.concatenate([jnp.zeros((device_count, 1), jnp.int32), cut_points, used_blocks], axis=1)
    block_counts = edges[:, 1:] - edges[:, :-1]
    tail_tokens = jax.random.randint(key_tail, (device_count, SEQS_DEV), 1, PAD_BLOCK + 1)
    length_table = jnp.where(block_counts > 0, (block_counts - 1) * PAD_BLOCK + tail_tokens, 0)
    chosen_device = jax.random.randint(key_pick, (), 0, device_count)
    full_row = jnp.where(jnp.arange(SEQS_DEV) == 0, TOKENS_PER_SHARD, 0).astype(jnp.int32)
    picked = (jnp.arange(device_count) == chosen_device)[:, None]
    length_table = jnp.where(picked, full_row[None, :], length_table)
    return length_table.reshape(-1).astype(jnp.int32)


def block_scale(own_key, extent, cuts, smallest, largest):
    def one(position, parts):
        draws = jax.random.uniform(jax.random.fold_in(jax.random.fold_in(own_key, 6), position), (parts,), jnp.float32, smallest / len(cuts), largest / len(cuts))
        return jnp.repeat(jnp.exp(draws), extent[position] // parts).reshape((-1,) + (1,) * (len(extent) - position - 1))

    gain = one(*cuts[0])
    for cut in cuts[1:]:
        gain = gain * one(*cut)
    return gain


def scatter_about(own_key, extent, scale, limit, shards=(), kind=jnp.bfloat16):
    level = block_scale(own_key, extent, shards, -0.22, 0.18) if shards else 1.0
    values = jax.random.normal(own_key, extent, jnp.float32) * scale * level
    return jnp.minimum(jnp.maximum(values, -limit), limit).astype(kind)


def setup_inputs(seed: int = 0) -> dict:
    splits = jax.random.split(jax.random.key(seed), 13)
    layer_input = scatter_about(splits[0], (TOKENS, D), 1.0, 6.0, ((0, 32),))
    seq_lengths = draw_seq_lengths(jax.random.fold_in(splits[12], 71), 0)
    out_cotangent = scatter_about(splits[2], (TOKENS, D), 1.0, 6.0, ((0, 32),))
    attn_gain = jnp.clip(1.0 + 0.18 * jax.random.normal(splits[3], (D,), jnp.float32), 0.099609375, 1.8984375).astype(jnp.bfloat16)
    w_query = scatter_about(splits[4], (D, D), D ** -0.5, 0.25, ((0, 2),))
    w_key = scatter_about(splits[5], (D, KV), D ** -0.5, 0.25, ((0, 2),))
    w_value = scatter_about(splits[6], (D, KV), D ** -0.5, 0.25, ((0, 2),))
    w_out = scatter_about(splits[7], (D, D), (HEAD_DIM // 4) ** -0.5, 1.5, ((0, 2),))
    mlp_gain = jnp.clip(1.0 + 0.18 * jax.random.normal(splits[8], (D,), jnp.float32), 0.099609375, 1.8984375).astype(jnp.bfloat16)
    w_gate = scatter_about(splits[9], (D, FF), D ** -0.5, 0.25, ((0, 2),))
    w_up = scatter_about(splits[10], (D, FF), D ** -0.5, 0.25, ((0, 2),))
    w_down = scatter_about(splits[11], (FF, D), FF ** -0.5, 0.15625, ((0, 2),))
    return dict(layer_input=layer_input, seq_lengths=seq_lengths, out_cotangent=out_cotangent, attn_gain=attn_gain, w_query=w_query, w_key=w_key, w_value=w_value, w_out=w_out, mlp_gain=mlp_gain, w_gate=w_gate, w_up=w_up, w_down=w_down)


norm_eps = 1e-05
rope_theta = 100000.0
masked_score = -1e+30

@jax.custom_vjp
def low(v):
    return lax.optimization_barrier(v.astype(jnp.bfloat16)).astype(jnp.float32)

@jax.custom_vjp
def low_back(v):
    return v

def low_keep(v):
    return (low(v), None)

def low_pass(kept, grad):
    return (grad,)

def back_keep(v):
    return (v, None)

def back_low(kept, grad):
    return (low(grad),)
low.defvjp(low_keep, low_pass)
low_back.defvjp(back_keep, back_low)

def layout(length_row, total_rows):
    block_count = (length_row + PAD_BLOCK - 1) // PAD_BLOCK
    stop_rows = (jnp.cumsum(block_count) * PAD_BLOCK).astype(jnp.int32)
    first_rows = (stop_rows - block_count * PAD_BLOCK).astype(jnp.int32)
    row_index = jnp.arange(total_rows, dtype=jnp.int32)
    inside = (row_index[:, None] >= first_rows[None, :]) & (row_index[:, None] < (first_rows + length_row)[None, :])
    slot_ids = jnp.arange(length_row.shape[0], dtype=jnp.int32)
    live_rows = jnp.any(inside, axis=1)
    slot_of_row = lax.optimization_barrier(jnp.sum(jnp.where(inside, slot_ids[None, :], 0), axis=1)).astype(jnp.int32)
    labels = jnp.where(live_rows, slot_of_row, -1).astype(jnp.int32)
    offsets = lax.optimization_barrier(jnp.sum(jnp.where(inside, row_index[:, None] - first_rows[None, :], 0), axis=1)).astype(jnp.int32)
    return (labels, live_rows, offsets)

def rotary_tables(offsets):
    half_dim = HEAD_DIM // 2
    exponent = jnp.arange(half_dim, dtype=jnp.float32) * (2.0 / HEAD_DIM)
    frequency = jnp.power(jnp.float32(rope_theta), -exponent)
    angles = offsets.astype(jnp.float32)[:, None] * frequency[None, :]
    return (jnp.cos(angles), jnp.sin(angles))

def rotate(flat_rows, cosine, sine):
    row_count = flat_rows.shape[0]
    half_dim = HEAD_DIM // 2
    head_view = flat_rows.reshape(row_count, -1, HEAD_DIM)
    first_half = head_view[:, :, :half_dim]
    second_half = head_view[:, :, half_dim:]
    cos_wide = cosine[:, None, :]
    sin_wide = sine[:, None, :]
    turned = jnp.concatenate([first_half * cos_wide - second_half * sin_wide, second_half * cos_wide + first_half * sin_wide], axis=2)
    return turned.reshape(row_count, -1)

def matmul(left, right):
    return jnp.dot(left, right, preferred_element_type=jnp.float32, precision=lax.Precision.HIGHEST)

def rms_scaled(values, gain_vec):
    factor = lax.rsqrt(lax.optimization_barrier(jnp.mean(values * values, axis=1, keepdims=True)) + norm_eps)
    return values * factor * gain_vec

def attention(queries, key_rows, value_rows, labels):
    row_count = queries.shape[0]
    block_of_rows = min(512, row_count)
    group_size = HEADS // KV_HEADS
    score_scale = 1.0 / math.sqrt(HEAD_DIM)
    key_head_stack = key_rows.reshape(row_count, KV_HEADS, HEAD_DIM)
    value_heads = value_rows.reshape(row_count, KV_HEADS, HEAD_DIM)

    def one_block(begin_row):
        query_rows = lax.dynamic_slice_in_dim(queries, begin_row, block_of_rows, 0).reshape(block_of_rows, KV_HEADS, group_size, HEAD_DIM)
        query_labels = lax.dynamic_slice_in_dim(labels, begin_row, block_of_rows, 0)
        scores = low_back(jnp.einsum('rkgd,tkd->kgrt', query_rows, key_head_stack, precision=lax.Precision.HIGHEST) * score_scale)
        query_index = begin_row + jnp.arange(block_of_rows, dtype=jnp.int32)
        key_index = jnp.arange(row_count, dtype=jnp.int32)
        allowed = (query_labels[:, None] == labels[None, :]) & (key_index[None, :] <= query_index[:, None])
        scores = jnp.where(allowed[None, None], scores, masked_score)
        row_top = lax.optimization_barrier(jnp.max(scores, axis=3, keepdims=True))
        exponent_rows = jnp.exp(scores - row_top)
        weights = low(exponent_rows / lax.optimization_barrier(jnp.sum(exponent_rows, axis=3, keepdims=True)))
        mixed_rows = jnp.einsum('kgrt,tkd->rkgd', weights, value_heads, precision=lax.Precision.HIGHEST)
        return mixed_rows.reshape(block_of_rows, HEADS * HEAD_DIM)
    starts = jnp.arange(row_count // block_of_rows, dtype=jnp.int32) * block_of_rows
    return lax.map(jax.checkpoint(one_block), starts).reshape(row_count, HEADS * HEAD_DIM)

def layer(inputs, params, labels, live_rows, cosine, sine):
    gain_one, query_w, key_w, value_w, out_w, gain_two, gate_w, up_w, down_w = params
    normed_one = low(rms_scaled(inputs, gain_one))
    queries = low(rotate(low_back(matmul(normed_one, query_w)), cosine, sine))
    key_rows = low(rotate(low_back(matmul(normed_one, key_w)), cosine, sine))
    value_rows = low(low_back(matmul(normed_one, value_w)))
    attended = low(low_back(attention(queries, key_rows, value_rows, labels)))
    middle = inputs + low_back(matmul(attended, out_w))
    normed_two = low(rms_scaled(middle, gain_two))
    gate_proj = low_back(matmul(normed_two, gate_w))
    up_proj = low_back(matmul(normed_two, up_w))
    hidden = low(jax.nn.silu(gate_proj) * up_proj)
    result = middle + low_back(matmul(hidden, down_w))
    return jnp.where(live_rows[:, None], result, 0.0)

def reference(layer_input, seq_lengths, out_cotangent, attn_gain, w_query, w_key, w_value, w_out, mlp_gain, w_gate, w_up, w_down):
    device_count = N_REP * N_SHARD
    weights = tuple((weight_arg.astype(jnp.float32) for weight_arg in (attn_gain, w_query, w_key, w_value, w_out, mlp_gain, w_gate, w_up, w_down)))
    inputs = layer_input.astype(jnp.float32).reshape(device_count, TOKENS_PER_SHARD, D)
    cotangents = out_cotangent.astype(jnp.float32).reshape(device_count, TOKENS_PER_SHARD, D)
    length_rows = seq_lengths.reshape(device_count, SEQS_DEV)

    def one_device(totals, slices):
        inputs_dev, cotangent_dev, lengths_dev = slices
        labels, live_rows, offsets = layout(lengths_dev, TOKENS_PER_SHARD)
        cosine, sine = rotary_tables(offsets)

        def forward(inputs_here, *params):
            return layer(inputs_here, params, labels, live_rows, cosine, sine)
        output, pullback = jax.vjp(forward, inputs_dev, *weights)
        gradients = pullback(cotangent_dev)
        new_totals = tuple((total_now + grad_now for total_now, grad_now in zip(totals, gradients[1:])))
        return (new_totals, (output.astype(jnp.bfloat16), gradients[0].astype(jnp.bfloat16)))
    zero_sums = tuple((jnp.zeros_like(weight_arg) for weight_arg in weights))
    grad_totals, (outputs, input_grads) = lax.scan(one_device, zero_sums, (inputs, cotangents, length_rows))
    return (outputs.reshape(TOKENS, D), input_grads.reshape(TOKENS, D), grad_totals[0], grad_totals[1], grad_totals[2], grad_totals[3], grad_totals[4], grad_totals[5], grad_totals[6], grad_totals[7], grad_totals[8])
```

```python
import functools

import jax
import jax.numpy as jnp
from jax import lax
from jax.experimental import pallas as pl
from jax.experimental.pallas import tpu as pltpu
from jax.sharding import PartitionSpec as P

HEADS = 9
KV_HEADS = 3
HEAD_DIM = 64
PAD_BLOCK = 128


norm_eps = 1e-05
rope_theta = 100000.0
masked_score = -1e30


def layout(length_row, total_rows):
    block_count = (length_row + PAD_BLOCK - 1) // PAD_BLOCK
    stop_rows = jnp.cumsum(block_count) * PAD_BLOCK
    first_rows = stop_rows - block_count * PAD_BLOCK
    row_index = jnp.arange(total_rows, dtype=jnp.int32)
    inside = (row_index[:, None] >= first_rows[None, :]) & (
        row_index[:, None] < (first_rows + length_row)[None, :]
    )
    slot_ids = jnp.arange(length_row.shape[0], dtype=jnp.int32)
    live_rows = jnp.any(inside, axis=1)
    slot_of_row = jnp.sum(jnp.where(inside, slot_ids[None, :], 0), axis=1)
    labels = jnp.where(live_rows, slot_of_row, -1)
    offsets = jnp.sum(jnp.where(inside, row_index[:, None] - first_rows[None, :], 0), axis=1)
    return (labels, live_rows, offsets)


def rotary_tables(offsets):
    half_dim = HEAD_DIM // 2
    exponent = jnp.arange(half_dim, dtype=jnp.float32) * (2.0 / HEAD_DIM)
    frequency = jnp.power(jnp.float32(rope_theta), -exponent)
    angles = offsets.astype(jnp.float32)[:, None] * frequency[None, :]
    return (jnp.cos(angles), jnp.sin(angles))

GROUP = HEADS // KV_HEADS
ATT_BLOCK = 256
F32 = jnp.float32
BF16 = jnp.bfloat16


def dot(left, right, left_dim=1, right_dim=0):
    return lax.dot_general(
        left, right, (((left_dim,), (right_dim,)), ((), ())), preferred_element_type=F32
    )


def swap_halves(rows):
    half = HEAD_DIM // 2
    return jnp.concatenate([rows[:, half:], rows[:, :half]], axis=1)


def unit_and_scale(rows):
    scale = lax.rsqrt(jnp.mean(rows * rows, axis=1, keepdims=True) + norm_eps)
    return rows * scale, scale


def allowed_block(label_col, label_row, begin, size):
    keys = begin + size
    shape = (size, keys)
    row = begin + lax.broadcasted_iota(jnp.int32, shape, 0)
    col = lax.broadcasted_iota(jnp.int32, shape, 1)
    return (label_col[begin:keys, :] == label_row[:, :keys]) & (col <= row)


def forward_kernel(
    x_ref, gain_ref, wqkv_ref, wout_ref, cos_ref, sin_ref, lcol_ref, lrow_ref,
    q_ref, k_ref, v_ref, att_ref, lse_ref, mid_ref, n1_ref,
):
    rows = x_ref.shape[0]

    @pl.when(pl.program_id(0) == 0)
    def _():
        x = x_ref[...].astype(F32)
        unit, _ = unit_and_scale(x)
        n1_ref[...] = (unit * gain_ref[...].astype(F32)).astype(BF16)
        mid_ref[...] = x

    proj = dot(n1_ref[...], wqkv_ref[0])
    cos, sin = cos_ref[...], sin_ref[...]
    for head in range(GROUP + 1):
        part = proj[:, head * HEAD_DIM : (head + 1) * HEAD_DIM]
        turned = part * cos + swap_halves(part) * sin
        if head < GROUP:
            q_ref[0, head] = (turned * (HEAD_DIM ** -0.5)).astype(BF16)
        else:
            k_ref[0] = turned.astype(BF16)
    v_ref[0] = proj[:, (GROUP + 1) * HEAD_DIM :].astype(BF16)
    for begin in range(0, rows, ATT_BLOCK):
        stop = begin + ATT_BLOCK
        allowed = allowed_block(lcol_ref, lrow_ref, begin, ATT_BLOCK)
        keys, values = k_ref[0, :stop, :], v_ref[0, :stop, :]
        for head in range(GROUP):
            scores = dot(q_ref[0, head, begin:stop, :], keys, 1, 1)
            scores = jnp.where(allowed, scores, masked_score)
            top = jnp.max(scores, axis=1, keepdims=True)
            weights = jnp.exp(scores - top)
            total = jnp.sum(weights, axis=1, keepdims=True)
            low = (weights * (1.0 / total)).astype(BF16)
            mixed = dot(low, values)
            att_ref[0, begin:stop, head * HEAD_DIM : (head + 1) * HEAD_DIM] = mixed.astype(BF16)
            lse_ref[0, begin:stop, head : head + 1] = top + jnp.log(total)
    mid_ref[...] += dot(att_ref[0], wout_ref[...])


def mlp_kernel(
    mid_ref, cot_ref, live_ref, gain_ref, wg_ref, wu_ref, wd_ref, att_ref,
    out_ref, gm_ref, gg_ref, gu_ref, gd_ref, go_ref, gain_grad_ref,
    n2_ref, low_ref, acc_ref, gn_ref,
):
    step = pl.program_id(0)

    @pl.when(step == 0)
    def _():
        unit, _ = unit_and_scale(mid_ref[...])
        n2_ref[...] = (unit * gain_ref[...].astype(F32)).astype(BF16)
        low_ref[...] = jnp.where(live_ref[...] > 0, cot_ref[...].astype(F32), 0.0).astype(BF16)
        acc_ref[...] = mid_ref[...]
        gn_ref[...] = jnp.zeros_like(gn_ref)

    n2, low = n2_ref[...], low_ref[...]
    gate = dot(n2, wg_ref[...])
    up = dot(n2, wu_ref[...])
    hidden_grad = dot(low, wd_ref[...], 1, 1)
    sig = jax.nn.sigmoid(gate)
    silu = gate * sig
    hidden = (silu * up).astype(BF16)
    up_grad = (hidden_grad * silu).astype(BF16)
    gate_grad = (hidden_grad * up * sig * (1.0 + gate * (1.0 - sig))).astype(BF16)
    acc_ref[...] += dot(hidden, wd_ref[...])
    gn_ref[...] += dot(gate_grad, wg_ref[...], 1, 1) + dot(up_grad, wu_ref[...], 1, 1)
    gd_ref[...] = dot(hidden, low, 0, 0).astype(BF16)
    gate_w = dot(n2, gate_grad, 0, 0).astype(BF16)
    up_w = dot(n2, up_grad, 0, 0).astype(BF16)
    width = gg_ref.shape[2]
    for part in range(gg_ref.shape[0]):
        gg_ref[part] = gate_w[:, part * width : (part + 1) * width]
        gu_ref[part] = up_w[:, part * width : (part + 1) * width]

    @pl.when(step == pl.num_programs(0) - 1)
    def _():
        live = live_ref[...] > 0
        out_ref[...] = jnp.where(live, acc_ref[...], 0.0).astype(BF16)
        unit, scale = unit_and_scale(mid_ref[...])
        grad = gn_ref[...]
        gain_grad_ref[...] = jnp.sum(grad * unit, axis=0, keepdims=True)
        scaled = grad * gain_ref[...].astype(F32)
        gm = low_ref[...].astype(F32) + scale * (
            scaled - unit * jnp.mean(scaled * unit, axis=1, keepdims=True)
        )
        gm_ref[...] = gm
        gm_low = gm.astype(BF16)
        piece = go_ref.shape[2]
        for group in range(KV_HEADS):
            block = dot(att_ref[group], gm_low, 0, 0)
            size = block.shape[0]
            for part in range(go_ref.shape[0]):
                go_ref[part, group * size : (group + 1) * size, :] = block[
                    :, part * piece : (part + 1) * piece
                ].astype(BF16)


def backward_kernel(
    x_ref, gain_ref, gm_ref, q_ref, k_ref, v_ref, lse_ref, wqkv_ref, wout_ref,
    cos_ref, sin_ref, lcol_ref, lrow_ref, gain_two_ref,
    xg_ref, gw_ref,
    n1_ref, low_ref, gn_ref, cat_ref, dk_ref, dv_ref,
):
    step = pl.program_id(0)
    rows = x_ref.shape[0]

    @pl.when(step == 0)
    def _():
        unit, _ = unit_and_scale(x_ref[...].astype(F32))
        n1_ref[...] = (unit * gain_ref[...].astype(F32)).astype(BF16)
        low_ref[...] = gm_ref[...].astype(BF16)
        gn_ref[...] = jnp.zeros_like(gn_ref)

    dk_ref[...] = jnp.zeros_like(dk_ref)
    dv_ref[...] = jnp.zeros_like(dv_ref)
    att_grad = dot(low_ref[...], wout_ref[...], 1, 1).astype(BF16)
    for begin in range(0, rows, ATT_BLOCK):
        stop = begin + ATT_BLOCK
        allowed = allowed_block(lcol_ref, lrow_ref, begin, ATT_BLOCK)
        keys, values = k_ref[0, :stop, :], v_ref[0, :stop, :]
        cos, sin = cos_ref[begin:stop, :], sin_ref[begin:stop, :]
        for head in range(GROUP):
            queries = q_ref[0, head, begin:stop, :]
            grads = att_grad[begin:stop, head * HEAD_DIM : (head + 1) * HEAD_DIM]
            scores = jnp.where(allowed, dot(queries, keys, 1, 1), masked_score)
            weights = jnp.exp(scores - lse_ref[0, begin:stop, head : head + 1])
            weight_grad = dot(grads, values, 1, 1)
            centre = jnp.sum(weights * weight_grad, axis=1, keepdims=True)
            score_grad = (weights * (weight_grad - centre)).astype(BF16)
            dk_ref[:stop, :] += dot(score_grad, queries, 0, 0)
            dv_ref[:stop, :] += dot(weights.astype(BF16), grads, 0, 0)
            dq = dot(score_grad, keys) * (HEAD_DIM ** -0.5)
            cat_ref[begin:stop, head * HEAD_DIM : (head + 1) * HEAD_DIM] = (
                dq * cos - swap_halves(dq) * sin
            ).astype(BF16)
    dk = dk_ref[...]
    cat_ref[:, GROUP * HEAD_DIM : (GROUP + 1) * HEAD_DIM] = (
        dk * cos_ref[...] - swap_halves(dk) * sin_ref[...]
    ).astype(BF16)
    cat_ref[:, (GROUP + 1) * HEAD_DIM :] = dv_ref[...].astype(BF16)
    gn_ref[...] += dot(cat_ref[...], wqkv_ref[0], 1, 1)
    grad_w = dot(n1_ref[...], cat_ref[...], 0, 0)
    piece = grad_w.shape[0] // 8
    for shard in range(2):
        for part in range(4):
            at = (shard * 4 + part) * piece
            gw_ref[part, shard, 0, :piece, :] = grad_w[at : at + piece].astype(BF16)
    gw_ref[:, :, :, piece:, :] = jnp.zeros_like(gw_ref[:, :, :, piece:, :])

    @pl.when(step == pl.num_programs(0) - 1)
    def _():
        unit, scale = unit_and_scale(x_ref[...].astype(F32))
        grad = gn_ref[...]
        gain_sum = jnp.sum(grad * unit, axis=0, keepdims=True)
        half = gain_sum.shape[1] // 2
        pad = jnp.zeros((6, half), F32)
        for shard in range(2):
            lanes = slice(shard * half, (shard + 1) * half)
            gw_ref[0, shard, 0, piece:, :half] = jnp.concatenate(
                [gain_sum[:, lanes], gain_two_ref[:, lanes], pad], axis=0
            ).astype(BF16)
        scaled = grad * gain_ref[...].astype(F32)
        xg_ref[...] = (
            gm_ref[...]
            + scale * (scaled - unit * jnp.mean(scaled * unit, axis=1, keepdims=True))
        ).astype(BF16)


def whole(shape):
    return pl.BlockSpec(shape, lambda i: (0,) * len(shape))


def lead(shape):
    return pl.BlockSpec(shape, lambda i: (i,) + (0,) * (len(shape) - 1))


def params(**more):
    return pltpu.CompilerParams(vmem_limit_bytes=56 * 1024 * 1024, **more)


def take(array, index, axis=0):
    return lax.dynamic_index_in_dim(array, index, axis, keepdims=False)


def swap(array, axis, size, bit):
    return lax.ppermute(array, axis, [(i, i ^ bit) for i in range(size)])


def halve(array, axis, size, bit, mine):
    sent = swap(take(array, 1 - mine), axis, size, bit)
    return (take(array, mine).astype(F32) + sent.astype(F32)).astype(BF16)


def both(array, other, mine):
    return jnp.where(mine == 0, jnp.stack([array, other]), jnp.stack([other, array]))


def reduce_pieces(array, core, x, shard, n_rep):
    array = halve(array, "rep", n_rep, 1, core)
    array = halve(jnp.swapaxes(array, 0, 1), "shard", 2, 1, shard)
    array = halve(array, "rep", n_rep, 2, x)
    bit = 4
    while bit < n_rep:
        array = (array.astype(F32) + swap(array, "rep", n_rep, bit).astype(F32)).astype(BF16)
        bit *= 2
    array = both(array, swap(array, "rep", n_rep, 2), x)
    return both(array, swap(array, "rep", n_rep, 1), core)


def gather_halves(first, second, core, shard, n_rep):
    got = swap(jnp.where(core == 0, first, second), "shard", 2, 1)
    other = swap(got, "rep", n_rep, 1)
    far_first = jnp.where(core == 0, got, other)
    far_second = jnp.where(core == 0, other, got)

    def join(near, far):
        return both(near, far, shard).reshape((-1,) + near.shape[1:])

    return join(first, far_first), join(second, far_second)


def local(
    n_rep, n_shard, layer_input, seq_lengths, out_cotangent, attn_gain, w_query, w_key, w_value,
    w_out, mlp_gain, w_gate, w_up, w_down,
):
    rows, width = layer_input.shape
    ff = w_gate.shape[1]
    group_width = GROUP * HEAD_DIM
    packed_width = group_width + 2 * HEAD_DIM
    quick = n_shard == 2 and n_rep >= 4 and n_rep & (n_rep - 1) == 0
    rep, shard = lax.axis_index("rep"), lax.axis_index("shard")
    core, x_bit = rep % 2, (rep // 2) % 2

    own_rows = w_query.shape[0]
    qkv = jnp.concatenate(
        [
            w_query.reshape(own_rows, KV_HEADS, group_width),
            w_key.reshape(own_rows, KV_HEADS, HEAD_DIM),
            w_value.reshape(own_rows, KV_HEADS, HEAD_DIM),
        ],
        axis=2,
    ).reshape(own_rows, -1)
    gains = jnp.concatenate([attn_gain, mlp_gain])[None, :]
    if quick:
        pack = jnp.concatenate(
            [
                jnp.concatenate([qkv, w_out], axis=1),
                jnp.pad(gains, ((0, 15), (0, qkv.shape[1] + w_out.shape[1] - gains.shape[1]))),
            ],
            axis=0,
        )
        middle = pack.shape[0] // 2
        top, low = gather_halves(pack[:middle], pack[middle:], core, shard, n_rep)
        top, low = top.reshape(2, middle, -1), low.reshape(2, middle, -1)
        packed = jnp.concatenate([top, low], axis=1)
        weights = packed[:, :own_rows].reshape(width, -1)
        gain_rows = packed[:, own_rows, : gains.shape[1]]
        gain_one = gain_rows[:, :own_rows].reshape(1, width)
        gain_two = gain_rows[:, own_rows:].reshape(1, width)
        qkv_full, out_full = weights[:, : qkv.shape[1]], weights[:, qkv.shape[1] :]
        gate_full, up_full = gather_halves(w_gate, w_up, core, shard, n_rep)
        down_half = w_down.shape[0] // 2
        top, low = gather_halves(w_down[:down_half], w_down[down_half:], core, shard, n_rep)
        down_full = jnp.concatenate(
            [top.reshape(2, down_half, width), low.reshape(2, down_half, width)], axis=1
        ).reshape(-1, width)
    else:
        gather = functools.partial(lax.all_gather, axis_name="shard", axis=0, tiled=True)
        qkv_full, out_full = gather(qkv), gather(w_out)
        gate_full, up_full, down_full = gather(w_gate), gather(w_up), gather(w_down)
        gain_one, gain_two = gather(attn_gain)[None], gather(mlp_gain)[None]
    qkv_full = qkv_full.reshape(width, KV_HEADS, packed_width).swapaxes(0, 1)

    labels, live_rows, offsets = layout(seq_lengths, rows)
    cosine, sine = rotary_tables(offsets)
    cos_full = jnp.concatenate([cosine, cosine], axis=1)
    sin_full = jnp.concatenate([-sine, sine], axis=1)
    label_col, label_row = labels[:, None], labels[None, :]
    live = live_rows.astype(F32)[:, None]

    shape = jax.ShapeDtypeStruct
    head_block = lead((1, GROUP, rows, HEAD_DIM))
    kv_block = lead((1, rows, HEAD_DIM))
    lse_block = lead((1, rows, GROUP))
    qkv_block = lead((1, width, packed_width))
    out_block = lead((group_width, width))
    tables = [whole((rows, HEAD_DIM))] * 2 + [whole((rows, 1)), whole((1, rows))]
    row_block, gain_block = whole((rows, width)), whole((1, width))
    queries, keys, values, attended, lse, middle = pl.pallas_call(
        forward_kernel,
        grid=(KV_HEADS,),
        in_specs=[row_block, gain_block, qkv_block, out_block] + tables,
        out_specs=[
            head_block, kv_block, kv_block, lead((1, rows, group_width)), lse_block, row_block,
        ],
        out_shape=[
            shape((KV_HEADS, GROUP, rows, HEAD_DIM), BF16),
            shape((KV_HEADS, rows, HEAD_DIM), BF16),
            shape((KV_HEADS, rows, HEAD_DIM), BF16),
            shape((KV_HEADS, rows, group_width), BF16),
            shape((KV_HEADS, rows, GROUP), F32),
            shape((rows, width), F32),
        ],
        scratch_shapes=[pltpu.VMEM((rows, width), BF16)],
        compiler_params=params(),
        cost_estimate=pl.CostEstimate(
            flops=30_000_000_000, bytes_accessed=20_000_000, transcendentals=6_000_000
        ),
        name="attention_forward",
    )(layer_input, gain_one, qkv_full, out_full, cos_full, sin_full, label_col, label_row)

    steps, parts = 2, 4
    chunk, per_step = ff // steps, parts // steps
    layer_output, gm, g_gate, g_up, g_down, g_out, g_gain = pl.pallas_call(
        mlp_kernel,
        grid=(steps,),
        in_specs=[
            row_block, row_block, whole((rows, 1)), gain_block,
            pl.BlockSpec((width, chunk), lambda i: (0, i)),
            pl.BlockSpec((width, chunk), lambda i: (0, i)),
            lead((chunk, width)),
            whole((KV_HEADS, rows, group_width)),
        ],
        out_specs=[
            row_block, row_block,
            lead((per_step, width, ff // parts)),
            lead((per_step, width, ff // parts)),
            lead((chunk, width)),
            whole((parts, width, width // parts)),
            gain_block,
        ],
        out_shape=[
            shape((rows, width), BF16),
            shape((rows, width), F32),
            shape((parts, width, ff // parts), BF16),
            shape((parts, width, ff // parts), BF16),
            shape((ff, width), BF16),
            shape((parts, width, width // parts), BF16),
            shape((1, width), F32),
        ],
        scratch_shapes=[
            pltpu.VMEM((rows, width), BF16),
            pltpu.VMEM((rows, width), BF16),
            pltpu.VMEM((rows, width), F32),
            pltpu.VMEM((rows, width), F32),
        ],
        compiler_params=params(),
        cost_estimate=pl.CostEstimate(
            flops=30_000_000_000, bytes_accessed=20_000_000, transcendentals=2_000_000
        ),
        name="mlp_both",
    )(middle, out_cotangent, live, gain_two, gate_full, up_full, down_full, attended)

    padded = width // 8 + 8
    input_grad, g_qkv = pl.pallas_call(
        backward_kernel,
        grid=(KV_HEADS,),
        in_specs=[
            row_block, gain_block, row_block, head_block, kv_block, kv_block, lse_block,
            qkv_block, out_block,
        ] + tables + [gain_block],
        out_specs=[
            row_block,
            pl.BlockSpec((4, 2, 1, padded, packed_width), lambda i: (0, 0, i, 0, 0)),
        ],
        out_shape=[
            shape((rows, width), BF16),
            shape((4, 2, KV_HEADS, padded, packed_width), BF16),
        ],
        scratch_shapes=[
            pltpu.VMEM((rows, width), BF16),
            pltpu.VMEM((rows, width), BF16),
            pltpu.VMEM((rows, width), F32),
            pltpu.VMEM((rows, packed_width), BF16),
            pltpu.VMEM((rows, HEAD_DIM), F32),
            pltpu.VMEM((rows, HEAD_DIM), F32),
        ],
        compiler_params=params(),
        cost_estimate=pl.CostEstimate(
            flops=60_000_000_000, bytes_accessed=20_000_000, transcendentals=6_000_000
        ),
        name="attention_backward",
    )(
        layer_input, gain_one, gm, queries, keys, values, lse, qkv_full, out_full,
        cos_full, sin_full, label_col, label_row, g_gain,
    )

    piece = width // 8
    half = width // 2
    if quick:
        sums = functools.partial(
            reduce_pieces, core=core, x=x_bit, shard=shard, n_rep=n_rep
        )
        down = g_down.reshape(2, 2, 2, ff // 8, width).transpose(1, 2, 0, 3, 4)
        down_final = sums(down).reshape(ff // 2, width)

        def lanes(array):
            got = sums(array.reshape(2, 2, 2, half, array.shape[2]))
            return got.reshape(4, half, -1).swapaxes(0, 1).reshape(half, -1)

        gate_final, up_final, out_final = lanes(g_gate), lanes(g_up), lanes(g_out)
        got = sums(g_qkv.reshape(2, 2, 2, KV_HEADS, padded, packed_width))
        got = got.reshape(4, KV_HEADS, padded, packed_width)
        gain_rows = got[0, KV_HEADS - 1, piece : piece + 2, :half]
        gain_one_final, gain_two_final = gain_rows[0], gain_rows[1]
        qkv_grad = got[:, :, :piece].swapaxes(1, 2).reshape(half, KV_HEADS, packed_width)
    else:
        def sums(array):
            owned = lax.psum_scatter(array, "shard", scatter_dimension=0, tiled=True)
            return lax.psum(owned, "rep")

        def lanes(array):
            return sums(array.swapaxes(0, 1).reshape(width, -1))

        down_final = sums(g_down)
        gate_final, up_final, out_final = lanes(g_gate), lanes(g_up), lanes(g_out)
        gain_rows = g_qkv[0, :, KV_HEADS - 1, piece : piece + 2, :half]
        gain_one_final = sums(gain_rows[:, 0].reshape(width))
        gain_two_final = sums(gain_rows[:, 1].reshape(width))
        qkv_grad = g_qkv[:, :, :, :piece].transpose(1, 0, 3, 2, 4)
        qkv_grad = sums(qkv_grad.reshape(width, KV_HEADS, packed_width))
    own = qkv_grad.shape[0]
    query_final = qkv_grad[:, :, :group_width].reshape(own, -1)
    key_final = qkv_grad[:, :, group_width : group_width + HEAD_DIM].reshape(own, -1)
    value_final = qkv_grad[:, :, group_width + HEAD_DIM :].reshape(own, -1)
    finals = (
        gain_one_final, query_final, key_final, value_final, out_final,
        gain_two_final, gate_final, up_final, down_final,
    )
    return (layer_output, input_grad) + tuple(final.astype(F32) for final in finals)


def solution(mesh):
    return jax.shard_map(
        functools.partial(local, mesh.shape["rep"], mesh.shape["shard"]),
        mesh=mesh,
        in_specs=(
            P(("rep", "shard"), None),
            P(("rep", "shard")),
            P(("rep", "shard"), None),
            P("shard"),
            P("shard", None),
            P("shard", None),
            P("shard", None),
            P("shard", None),
            P("shard"),
            P("shard", None),
            P("shard", None),
            P("shard", None),
        ),
        out_specs=(
            P(("rep", "shard"), None),
            P(("rep", "shard"), None),
            P("shard"),
            P("shard", None),
            P("shard", None),
            P("shard", None),
            P("shard", None),
            P("shard"),
            P("shard", None),
            P("shard", None),
            P("shard", None),
        ),
        check_vma=False,
    )
```

```python
import functools

import jax
import jax.numpy as jnp
from jax import lax
from jax.experimental import pallas as pl
from jax.experimental.pallas import tpu as pltpu
from jax.sharding import PartitionSpec as P

HEADS = 9
KV_HEADS = 3
HEAD_DIM = 64
PAD_BLOCK = 128


norm_eps = 1e-05
rope_theta = 100000.0
masked_score = -1e30


def layout(length_row, total_rows):
    block_count = (length_row + PAD_BLOCK - 1) // PAD_BLOCK
    stop_rows = jnp.cumsum(block_count) * PAD_BLOCK
    first_rows = stop_rows - block_count * PAD_BLOCK
    row_index = jnp.arange(total_rows, dtype=jnp.int32)
    inside = (row_index[:, None] >= first_rows[None, :]) & (
        row_index[:, None] < (first_rows + length_row)[None, :]
    )
    slot_ids = jnp.arange(length_row.shape[0], dtype=jnp.int32)
    live_rows = jnp.any(inside, axis=1)
    slot_of_row = jnp.sum(jnp.where(inside, slot_ids[None, :], 0), axis=1)
    labels = jnp.where(live_rows, slot_of_row, -1)
    offsets = jnp.sum(jnp.where(inside, row_index[:, None] - first_rows[None, :], 0), axis=1)
    return (labels, live_rows, offsets)


def rotary_tables(offsets):
    half_dim = HEAD_DIM // 2
    exponent = jnp.arange(half_dim, dtype=jnp.float32) * (2.0 / HEAD_DIM)
    frequency = jnp.power(jnp.float32(rope_theta), -exponent)
    angles = offsets.astype(jnp.float32)[:, None] * frequency[None, :]
    return (jnp.cos(angles), jnp.sin(angles))

GROUP = HEADS // KV_HEADS
ATT_BLOCK = 256
F32 = jnp.float32
BF16 = jnp.bfloat16


def dot(left, right, left_dim=1, right_dim=0):
    return lax.dot_general(
        left, right, (((left_dim,), (right_dim,)), ((), ())), preferred_element_type=F32
    )


def swap_halves(rows):
    half = HEAD_DIM // 2
    return jnp.concatenate([rows[:, half:], rows[:, :half]], axis=1)


def unit_and_scale(rows):
    scale = lax.rsqrt(jnp.mean(rows * rows, axis=1, keepdims=True) + norm_eps)
    return rows * scale, scale


def allowed_block(label_col, label_row, begin, size):
    keys = begin + size
    shape = (size, keys)
    row = begin + lax.broadcasted_iota(jnp.int32, shape, 0)
    col = lax.broadcasted_iota(jnp.int32, shape, 1)
    return (label_col[begin:keys, :] == label_row[:, :keys]) & (col <= row)


def forward_kernel(
    x_ref, gain_ref, wqkv_ref, wout_ref, cos_ref, sin_ref, lcol_ref, lrow_ref,
    q_ref, k_ref, v_ref, att_ref, lse_ref, mid_ref, n1_ref,
):
    rows = x_ref.shape[0]

    @pl.when(pl.program_id(0) == 0)
    def _():
        x = x_ref[...].astype(F32)
        unit, _ = unit_and_scale(x)
        n1_ref[...] = (unit * gain_ref[...].astype(F32)).astype(BF16)
        mid_ref[...] = x

    proj = dot(n1_ref[...], wqkv_ref[0])
    cos, sin = cos_ref[...], sin_ref[...]
    for head in range(GROUP + 1):
        part = proj[:, head * HEAD_DIM : (head + 1) * HEAD_DIM]
        turned = part * cos + swap_halves(part) * sin
        if head < GROUP:
            q_ref[0, head] = (turned * (HEAD_DIM ** -0.5)).astype(BF16)
        else:
            k_ref[0] = turned.astype(BF16)
    v_ref[0] = proj[:, (GROUP + 1) * HEAD_DIM :].astype(BF16)
    for begin in range(0, rows, ATT_BLOCK):
        stop = begin + ATT_BLOCK
        allowed = allowed_block(lcol_ref, lrow_ref, begin, ATT_BLOCK)
        keys, values = k_ref[0, :stop, :], v_ref[0, :stop, :]
        for head in range(GROUP):
            scores = dot(q_ref[0, head, begin:stop, :], keys, 1, 1)
            scores = jnp.where(allowed, scores, masked_score)
            top = jnp.max(scores, axis=1, keepdims=True)
            weights = jnp.exp(scores - top)
            total = jnp.sum(weights, axis=1, keepdims=True)
            low = (weights * (1.0 / total)).astype(BF16)
            mixed = dot(low, values)
            att_ref[0, begin:stop, head * HEAD_DIM : (head + 1) * HEAD_DIM] = mixed.astype(BF16)
            lse_ref[0, begin:stop, head : head + 1] = top + jnp.log(total)
    mid_ref[...] += dot(att_ref[0], wout_ref[...])


def mlp_kernel(
    mid_ref, cot_ref, live_ref, gain_ref, wg_ref, wu_ref, wd_ref, att_ref,
    out_ref, gm_ref, ga_ref, gb_ref, gain_grad_ref,
    n2_ref, low_ref, acc_ref, gn_ref,
):
    step = pl.program_id(0)

    @pl.when(step == 0)
    def _():
        unit, _ = unit_and_scale(mid_ref[...])
        n2_ref[...] = (unit * gain_ref[...].astype(F32)).astype(BF16)
        low_ref[...] = jnp.where(live_ref[...] > 0, cot_ref[...].astype(F32), 0.0).astype(BF16)
        acc_ref[...] = mid_ref[...]
        gn_ref[...] = jnp.zeros_like(gn_ref)

    n2, low = n2_ref[...], low_ref[...]
    gate = dot(n2, wg_ref[...])
    up = dot(n2, wu_ref[...])
    hidden_grad = dot(low, wd_ref[...], 1, 1)
    sig = jax.nn.sigmoid(gate)
    silu = gate * sig
    hidden = (silu * up).astype(BF16)
    up_grad = (hidden_grad * silu).astype(BF16)
    gate_grad = (hidden_grad * up * sig * (1.0 + gate * (1.0 - sig))).astype(BF16)
    acc_ref[...] += dot(hidden, wd_ref[...])
    gn_ref[...] += dot(gate_grad, wg_ref[...], 1, 1) + dot(up_grad, wu_ref[...], 1, 1)
    rows, lanes = ga_ref.shape[2] // 2, ga_ref.shape[3]
    gate_w = dot(n2, gate_grad, 0, 0).astype(BF16)
    up_w = dot(n2, up_grad, 0, 0).astype(BF16)
    for part in range(2):
        for shard in range(2):
            at = (slice(shard * rows, (shard + 1) * rows), slice(part * lanes, (part + 1) * lanes))
            ga_ref[2 * step + part, shard, :rows, :] = gate_w[at]
            ga_ref[2 * step + part, shard, rows:, :] = up_w[at]
    down_w = dot(hidden, low, 0, 0).astype(BF16)
    size = down_w.shape[0] // 4
    for part in range(4):
        block = down_w[part * size : (part + 1) * size]
        gb_ref[part, step, :size, :] = block[:, :lanes]
        gb_ref[part, step, size : size + size // 2, : lanes // 2] = block[: size // 2, lanes:]
        gb_ref[part, step, size : size + size // 2, lanes // 2 :] = block[size // 2 :, lanes:]

    @pl.when(step == pl.num_programs(0) - 1)
    def _():
        live = live_ref[...] > 0
        out_ref[...] = jnp.where(live, acc_ref[...], 0.0).astype(BF16)
        unit, scale = unit_and_scale(mid_ref[...])
        grad = gn_ref[...]
        gain_grad_ref[...] = jnp.sum(grad * unit, axis=0, keepdims=True)
        scaled = grad * gain_ref[...].astype(F32)
        gm = low_ref[...].astype(F32) + scale * (
            scaled - unit * jnp.mean(scaled * unit, axis=1, keepdims=True)
        )
        gm_ref[...] = gm
        gm_low = gm.astype(BF16)
        grads = [dot(att_ref[group], gm_low, 0, 0) for group in range(KV_HEADS)]
        grads = jnp.concatenate(grads, axis=0)
        piece = grads.shape[0] // 8
        base = size + size // 2
        extra = jnp.zeros((8, grads.shape[1]), F32)
        side = jnp.zeros((piece + 8, 2 * lanes - grads.shape[1]), F32)
        for shard in range(2):
            for part in range(4):
                at = (shard * 4 + part) * piece
                block = jnp.concatenate([grads[at : at + piece], extra], axis=0)
                wide = jnp.concatenate([block[:, lanes:], side], axis=1)
                gb_ref[part, shard, base : base + piece + 8, :] = block[:, :lanes].astype(BF16)
                gb_ref[part, shard, base + piece + 8 :, :] = wide.astype(BF16)


def backward_kernel(
    first, last, x_ref, gain_ref, gm_ref, q_ref, k_ref, v_ref, lse_ref, wqkv_ref, wout_ref,
    cos_ref, sin_ref, lcol_ref, lrow_ref, gain_two_ref, gn_in_ref, after_a_ref, after_b_ref,
    xg_ref, gw_ref,
    n1_ref, low_ref, gn_ref, cat_ref, dk_ref, dv_ref,
):
    rows = x_ref.shape[0]
    unit, scale = unit_and_scale(x_ref[...].astype(F32))
    n1_ref[...] = (unit * gain_ref[...].astype(F32)).astype(BF16)
    low_ref[...] = gm_ref[...].astype(BF16)
    dk_ref[...] = jnp.zeros_like(dk_ref)
    dv_ref[...] = jnp.zeros_like(dv_ref)
    att_grad = dot(low_ref[...], wout_ref[...], 1, 1).astype(BF16)
    for begin in range(0, rows, ATT_BLOCK):
        stop = begin + ATT_BLOCK
        allowed = allowed_block(lcol_ref, lrow_ref, begin, ATT_BLOCK)
        keys, values = k_ref[0, :stop, :], v_ref[0, :stop, :]
        cos, sin = cos_ref[begin:stop, :], sin_ref[begin:stop, :]
        for head in range(GROUP):
            queries = q_ref[0, head, begin:stop, :]
            grads = att_grad[begin:stop, head * HEAD_DIM : (head + 1) * HEAD_DIM]
            scores = jnp.where(allowed, dot(queries, keys, 1, 1), masked_score)
            weights = jnp.exp(scores - lse_ref[0, begin:stop, head : head + 1])
            weight_grad = dot(grads, values, 1, 1)
            centre = jnp.sum(weights * weight_grad, axis=1, keepdims=True)
            score_grad = (weights * (weight_grad - centre)).astype(BF16)
            dk_ref[:stop, :] += dot(score_grad, queries, 0, 0)
            dv_ref[:stop, :] += dot(weights.astype(BF16), grads, 0, 0)
            dq = dot(score_grad, keys) * (HEAD_DIM ** -0.5)
            cat_ref[begin:stop, head * HEAD_DIM : (head + 1) * HEAD_DIM] = (
                dq * cos - swap_halves(dq) * sin
            ).astype(BF16)
    dk = dk_ref[...]
    cat_ref[:, GROUP * HEAD_DIM : (GROUP + 1) * HEAD_DIM] = (
        dk * cos_ref[...] - swap_halves(dk) * sin_ref[...]
    ).astype(BF16)
    cat_ref[:, (GROUP + 1) * HEAD_DIM :] = dv_ref[...].astype(BF16)
    gn_ref[...] = dot(cat_ref[...], wqkv_ref[0], 1, 1)
    if not first:
        gn_ref[...] += gn_in_ref[...]
    grad_w = dot(n1_ref[...], cat_ref[...], 0, 0)
    piece = grad_w.shape[0] // 8
    half = piece * 4
    for shard in range(2):
        tail = jnp.zeros((8, grad_w.shape[1]), F32)
        if last:
            grad = gn_ref[...]
            unit, scale = unit_and_scale(x_ref[...].astype(F32))
            cut = slice(shard * half, (shard + 1) * half)
            gain_sum = jnp.sum(grad * unit, axis=0, keepdims=True)
            tail = jnp.concatenate(
                [gain_sum[:, cut], gain_two_ref[:, cut], jnp.zeros((6, half), F32)], axis=0
            )
            tail = jnp.concatenate([tail, jnp.zeros((8, grad_w.shape[1] - half), F32)], axis=1)
        for part in range(4):
            at = (shard * 4 + part) * piece
            block = jnp.concatenate([grad_w[at : at + piece], tail], axis=0)
            gw_ref[part, shard] = block.astype(BF16)
    if last:
        unit, scale = unit_and_scale(x_ref[...].astype(F32))
        scaled = gn_ref[...] * gain_ref[...].astype(F32)
        xg_ref[...] = (
            gm_ref[...]
            + scale * (scaled - unit * jnp.mean(scaled * unit, axis=1, keepdims=True))
        ).astype(BF16)
    else:
        xg_ref[...] = gn_ref[...]


def assemble_kernel(shard_ref, q_ref, k_ref, v_ref, o_ref, far_ref, qkv_ref, out_ref):
    rows = q_ref.shape[0]
    shard = shard_ref[0]
    starts = (0, q_ref.shape[1], q_ref.shape[1] + k_ref.shape[1])
    starts = starts + (starts[2] + v_ref.shape[1],)

    def put(at, parts, out):
        where = slice(at * rows, (at + 1) * rows)
        out_ref[where, :] = out
        for group in range(KV_HEADS):
            begin = 0
            for part, size in zip(parts, (GROUP * HEAD_DIM, HEAD_DIM, HEAD_DIM)):
                qkv_ref[group, where, begin : begin + size] = part[
                    :, group * size : (group + 1) * size
                ]
                begin += size

    for near in range(2):

        @pl.when(shard == near)
        def _():
            put(near, (q_ref[...], k_ref[...], v_ref[...]), o_ref[...])
            far = far_ref[...]
            pieces = tuple(far[:, starts[i] : starts[i + 1]] for i in range(3))
            put(1 - near, pieces, far[:, starts[3] :])


def whole(shape):
    return pl.BlockSpec(shape, lambda i: (0,) * len(shape))


def lead(shape):
    return pl.BlockSpec(shape, lambda i: (i,) + (0,) * (len(shape) - 1))


def params(**more):
    return pltpu.CompilerParams(vmem_limit_bytes=60 * 1024 * 1024, **more)


def take(array, index, axis=0):
    return lax.dynamic_index_in_dim(array, index, axis, keepdims=False)


def swap(array, axis, size, bit):
    return lax.ppermute(array, axis, [(i, i ^ bit) for i in range(size)])


def halve(array, axis, size, bit, mine):
    sent = swap(take(array, 1 - mine), axis, size, bit)
    return (take(array, mine).astype(F32) + sent.astype(F32)).astype(BF16)


def both(array, other, mine):
    return jnp.where(mine == 0, jnp.stack([array, other]), jnp.stack([other, array]))


def reduce_steps(array, core, x, shard, n_rep, shard_first):
    array = halve(array, "rep", n_rep, 1, core)
    yield array
    if shard_first:
        array = halve(jnp.swapaxes(array, 0, 1), "shard", 2, 1, shard)
        yield array
        array = halve(array, "rep", n_rep, 2, x)
    else:
        array = halve(array, "rep", n_rep, 2, x)
        yield array
        array = halve(array, "shard", 2, 1, shard)
    yield array
    bit = 4
    while bit < n_rep:
        array = (array.astype(F32) + swap(array, "rep", n_rep, bit).astype(F32)).astype(BF16)
        bit *= 2
    array = both(array, swap(array, "rep", n_rep, 2), x)
    array = both(array, swap(array, "rep", n_rep, 1), core)
    yield array.reshape((4,) + array.shape[2:])


def gather_halves(first, second, core, shard, n_rep):
    got = swap(jnp.where(core == 0, first, second), "shard", 2, 1)
    other = swap(got, "rep", n_rep, 1)
    far_first = jnp.where(core == 0, got, other)
    far_second = jnp.where(core == 0, other, got)

    def join(near, far):
        return both(near, far, shard).reshape((-1,) + near.shape[1:])

    return join(first, far_first), join(second, far_second)


def local(
    n_rep, n_shard, layer_input, seq_lengths, out_cotangent, attn_gain, w_query, w_key, w_value,
    w_out, mlp_gain, w_gate, w_up, w_down,
):
    rows, width = layer_input.shape
    ff = w_gate.shape[1]
    group_width = GROUP * HEAD_DIM
    packed_width = group_width + 2 * HEAD_DIM
    quick = n_shard == 2 and n_rep >= 4 and n_rep & (n_rep - 1) == 0
    rep, shard = lax.axis_index("rep"), lax.axis_index("shard")
    core, x_bit = rep % 2, (rep // 2) % 2

    own_rows = w_query.shape[0]
    if quick:
        pack = jnp.concatenate([w_query, w_key, w_value, w_out], axis=1)
        far = swap(pack, "shard", 2, 1)
        gains = jnp.stack([attn_gain, mlp_gain])
        far_gains = swap(gains, "shard", 2, 1)
        gains = both(gains, far_gains, shard).swapaxes(0, 1).reshape(2, width)
        gain_one, gain_two = gains[:1], gains[1:]
        qkv_full, out_full = pl.pallas_call(
            assemble_kernel,
            in_specs=[pl.BlockSpec(memory_space=pltpu.SMEM)]
            + [pl.BlockSpec(memory_space=pltpu.VMEM)] * 5,
            out_specs=[pl.BlockSpec(memory_space=pltpu.VMEM)] * 2,
            out_shape=[
                jax.ShapeDtypeStruct((KV_HEADS, width, packed_width), BF16),
                jax.ShapeDtypeStruct((width, width), BF16),
            ],
            compiler_params=params(),
            name="assemble",
        )(shard[None], w_query, w_key, w_value, w_out, far)
        gate_full, up_full = gather_halves(w_gate, w_up, core, shard, n_rep)
        down_half = w_down.shape[0] // 2
        top, low = gather_halves(w_down[:down_half], w_down[down_half:], core, shard, n_rep)
        down_full = jnp.concatenate(
            [top.reshape(2, down_half, width), low.reshape(2, down_half, width)], axis=1
        ).reshape(-1, width)
    else:
        gather = functools.partial(lax.all_gather, axis_name="shard", axis=0, tiled=True)
        qkv = jnp.concatenate(
            [
                w_query.reshape(own_rows, KV_HEADS, group_width),
                w_key.reshape(own_rows, KV_HEADS, HEAD_DIM),
                w_value.reshape(own_rows, KV_HEADS, HEAD_DIM),
            ],
            axis=2,
        ).reshape(own_rows, -1)
        qkv_full, out_full = gather(qkv), gather(w_out)
        qkv_full = qkv_full.reshape(width, KV_HEADS, packed_width).swapaxes(0, 1)
        gate_full, up_full, down_full = gather(w_gate), gather(w_up), gather(w_down)
        gain_one, gain_two = gather(attn_gain)[None], gather(mlp_gain)[None]

    labels, live_rows, offsets = layout(seq_lengths, rows)
    cosine, sine = rotary_tables(offsets)
    cos_full = jnp.concatenate([cosine, cosine], axis=1)
    sin_full = jnp.concatenate([-sine, sine], axis=1)
    label_col, label_row = labels[:, None], labels[None, :]
    live = live_rows.astype(F32)[:, None]

    shape = jax.ShapeDtypeStruct
    head_block = lead((1, GROUP, rows, HEAD_DIM))
    kv_block = lead((1, rows, HEAD_DIM))
    lse_block = lead((1, rows, GROUP))
    qkv_block = lead((1, width, packed_width))
    out_block = lead((group_width, width))
    tables = [whole((rows, HEAD_DIM))] * 2 + [whole((rows, 1)), whole((1, rows))]
    row_block, gain_block = whole((rows, width)), whole((1, width))
    queries, keys, values, attended, lse, middle = pl.pallas_call(
        forward_kernel,
        grid=(KV_HEADS,),
        in_specs=[row_block, gain_block, qkv_block, out_block] + tables,
        out_specs=[
            head_block, kv_block, kv_block, lead((1, rows, group_width)), lse_block, row_block,
        ],
        out_shape=[
            shape((KV_HEADS, GROUP, rows, HEAD_DIM), BF16),
            shape((KV_HEADS, rows, HEAD_DIM), BF16),
            shape((KV_HEADS, rows, HEAD_DIM), BF16),
            shape((KV_HEADS, rows, group_width), BF16),
            shape((KV_HEADS, rows, GROUP), F32),
            shape((rows, width), F32),
        ],
        scratch_shapes=[pltpu.VMEM((rows, width), BF16)],
        compiler_params=params(),
        cost_estimate=pl.CostEstimate(
            flops=30_000_000_000, bytes_accessed=20_000_000, transcendentals=6_000_000
        ),
        name="attention_forward",
    )(layer_input, gain_one, qkv_full, out_full, cos_full, sin_full, label_col, label_row)

    steps, parts = 2, 4
    chunk, per_step = ff // steps, parts // steps
    lanes = ff // parts
    piece, half = width // 8, width // 2
    b_rows = ff // 8 + ff // 16 + 2 * (piece + 8)
    layer_output, gm, g_a, g_b, g_gain = pl.pallas_call(
        mlp_kernel,
        grid=(steps,),
        in_specs=[
            row_block, row_block, whole((rows, 1)), gain_block,
            pl.BlockSpec((width, chunk), lambda i: (0, i)),
            pl.BlockSpec((width, chunk), lambda i: (0, i)),
            lead((chunk, width)),
            whole((KV_HEADS, rows, group_width)),
        ],
        out_specs=[
            row_block, row_block,
            whole((parts, 2, width, lanes)),
            whole((parts, 2, b_rows, lanes)),
            gain_block,
        ],
        out_shape=[
            shape((rows, width), BF16),
            shape((rows, width), F32),
            shape((parts, 2, width, lanes), BF16),
            shape((parts, 2, b_rows, lanes), BF16),
            shape((1, width), F32),
        ],
        scratch_shapes=[
            pltpu.VMEM((rows, width), BF16),
            pltpu.VMEM((rows, width), BF16),
            pltpu.VMEM((rows, width), F32),
            pltpu.VMEM((rows, width), F32),
        ],
        compiler_params=params(),
        cost_estimate=pl.CostEstimate(
            flops=30_000_000_000, bytes_accessed=20_000_000, transcendentals=2_000_000
        ),
        name="mlp_both",
    )(middle, out_cotangent, live, gain_two, gate_full, up_full, down_full, attended)

    padded = piece + 8
    g_parts = []
    carried = jnp.zeros((8, 128), F32)

    def steps_of(array, shard_first):
        array = array.reshape((2, 2) + array.shape[1:])
        return reduce_steps(array, core, x_bit, shard, n_rep, shard_first)

    if quick:
        steps_a, steps_b = steps_of(g_a, True), steps_of(g_b, False)
    after = (jnp.zeros((8, 128), BF16),) * 2
    for group in range(KV_HEADS):
        first, last = group == 0, group == KV_HEADS - 1

        def at_group(block, group=group):
            return pl.BlockSpec(block, lambda i: (group,) + (0,) * (len(block) - 1))

        carried, g_part = pl.pallas_call(
            functools.partial(backward_kernel, first, last),
            grid=(1,),
            in_specs=[
                row_block, gain_block, row_block,
                at_group((1, GROUP, rows, HEAD_DIM)), at_group((1, rows, HEAD_DIM)),
                at_group((1, rows, HEAD_DIM)), at_group((1, rows, GROUP)),
                at_group((1, width, packed_width)), at_group((group_width, width)),
            ] + tables + [gain_block, whole(carried.shape)]
            + [pl.BlockSpec(memory_space=pl.ANY)] * 2,
            out_specs=[row_block, whole((4, 2, padded, packed_width))],
            out_shape=[
                shape((rows, width), BF16 if last else F32),
                shape((4, 2, padded, packed_width), BF16),
            ],
            scratch_shapes=[
                pltpu.VMEM((rows, width), BF16),
                pltpu.VMEM((rows, width), BF16),
                pltpu.VMEM((rows, width), F32),
                pltpu.VMEM((rows, packed_width), BF16),
                pltpu.VMEM((rows, HEAD_DIM), F32),
                pltpu.VMEM((rows, HEAD_DIM), F32),
            ],
            compiler_params=params(),
            cost_estimate=pl.CostEstimate(
                flops=15_000_000_000, bytes_accessed=12_000_000, transcendentals=2_000_000
            ),
            name="attention_backward",
        )(
            layer_input, gain_one, gm, queries, keys, values, lse, qkv_full, out_full,
            cos_full, sin_full, label_col, label_row, g_gain, carried, *after,
        )
        if quick:
            after = (next(steps_a), next(steps_b))
        g_parts.append(g_part)
    input_grad = carried
    g_qkv = jnp.stack(g_parts, axis=2)

    def columns(array):
        array = jnp.moveaxis(array, 0, -2)
        return array.reshape(-1, ff)

    def unfold(array):
        cut = ff // 8
        left, right = array[..., :cut, :], array[..., cut : cut + cut // 2, :]
        right = jnp.concatenate([right[..., : lanes // 2], right[..., lanes // 2 :]], axis=-2)
        down = jnp.concatenate([left, right], axis=-1)
        at = cut + cut // 2
        left = array[..., at : at + piece, :]
        right = array[..., at + piece + 8 : at + 2 * piece + 8, : width - lanes]
        return down, jnp.concatenate([left, right], axis=-1)

    if quick:
        *_, got = steps_of(g_qkv, True)
        b_own, a_own = next(steps_b), next(steps_a)
        gate_final, up_final = columns(a_own[:, :half]), columns(a_own[:, half:])
        down_own, out_own = unfold(b_own)
        down_final, out_final = down_own.reshape(-1, width), out_own.reshape(-1, width)
        gain_rows = got[0, KV_HEADS - 1, piece : piece + 2, :half]
        gain_one_final, gain_two_final = gain_rows[0], gain_rows[1]
        qkv_grad = got[:, :, :piece].swapaxes(1, 2).reshape(half, KV_HEADS, packed_width)
    else:
        def sums(array):
            owned = lax.psum_scatter(array, "shard", scatter_dimension=0, tiled=True)
            return lax.psum(owned, "rep")

        gate_final, up_final = sums(columns(g_a[:, :, :half])), sums(columns(g_a[:, :, half:]))
        down_all, out_all = unfold(jnp.swapaxes(g_b, 0, 1))
        down_final, out_final = sums(down_all.reshape(ff, width)), sums(out_all.reshape(width, width))
        gain_rows = g_qkv[0, :, KV_HEADS - 1, piece : piece + 2, :half]
        gain_one_final = sums(gain_rows[:, 0].reshape(width))
        gain_two_final = sums(gain_rows[:, 1].reshape(width))
        qkv_grad = g_qkv[:, :, :, :piece].transpose(1, 0, 3, 2, 4)
        qkv_grad = sums(qkv_grad.reshape(width, KV_HEADS, packed_width))
    own = qkv_grad.shape[0]
    query_final = qkv_grad[:, :, :group_width].reshape(own, -1)
    key_final = qkv_grad[:, :, group_width : group_width + HEAD_DIM].reshape(own, -1)
    value_final = qkv_grad[:, :, group_width + HEAD_DIM :].reshape(own, -1)
    finals = (
        gain_one_final, query_final, key_final, value_final, out_final,
        gain_two_final, gate_final, up_final, down_final,
    )
    return (layer_output, input_grad) + tuple(final.astype(F32) for final in finals)


def solution(mesh):
    return jax.shard_map(
        functools.partial(local, mesh.shape["rep"], mesh.shape["shard"]),
        mesh=mesh,
        in_specs=(
            P(("rep", "shard"), None),
            P(("rep", "shard")),
            P(("rep", "shard"), None),
            P("shard"),
            P("shard", None),
            P("shard", None),
            P("shard", None),
            P("shard", None),
            P("shard"),
            P("shard", None),
            P("shard", None),
            P("shard", None),
        ),
        out_specs=(
            P(("rep", "shard"), None),
            P(("rep", "shard"), None),
            P("shard"),
            P("shard", None),
            P("shard", None),
            P("shard", None),
            P("shard", None),
            P("shard"),
            P("shard", None),
            P("shard", None),
            P("shard", None),
        ),
        check_vma=False,
    )
```

```python
import functools

import jax
import jax.numpy as jnp
from jax import lax
from jax.experimental import pallas as pl
from jax.experimental.pallas import tpu as pltpu
from jax.sharding import PartitionSpec as P

HEADS = 9
KV_HEADS = 3
HEAD_DIM = 64
PAD_BLOCK = 128


norm_eps = 1e-05
rope_theta = 100000.0
masked_score = -1e30


def layout(length_row, total_rows):
    block_count = (length_row + PAD_BLOCK - 1) // PAD_BLOCK
    stop_rows = jnp.cumsum(block_count) * PAD_BLOCK
    first_rows = stop_rows - block_count * PAD_BLOCK
    row_index = jnp.arange(total_rows, dtype=jnp.int32)
    inside = (row_index[:, None] >= first_rows[None, :]) & (
        row_index[:, None] < (first_rows + length_row)[None, :]
    )
    slot_ids = jnp.arange(length_row.shape[0], dtype=jnp.int32)
    live_rows = jnp.any(inside, axis=1)
    slot_of_row = jnp.sum(jnp.where(inside, slot_ids[None, :], 0), axis=1)
    labels = jnp.where(live_rows, slot_of_row, -1)
    offsets = jnp.sum(jnp.where(inside, row_index[:, None] - first_rows[None, :], 0), axis=1)
    return (labels, live_rows, offsets)


def rotary_tables(offsets):
    half_dim = HEAD_DIM // 2
    exponent = jnp.arange(half_dim, dtype=jnp.float32) * (2.0 / HEAD_DIM)
    frequency = jnp.power(jnp.float32(rope_theta), -exponent)
    angles = offsets.astype(jnp.float32)[:, None] * frequency[None, :]
    return (jnp.cos(angles), jnp.sin(angles))

GROUP = HEADS // KV_HEADS
ATT_BLOCK = 256
F32 = jnp.float32
BF16 = jnp.bfloat16


def dot(left, right, left_dim=1, right_dim=0):
    return lax.dot_general(
        left, right, (((left_dim,), (right_dim,)), ((), ())), preferred_element_type=F32
    )


def swap_halves(rows):
    half = HEAD_DIM // 2
    return jnp.concatenate([rows[:, half:], rows[:, :half]], axis=1)


def unit_and_scale(rows):
    scale = lax.rsqrt(jnp.mean(rows * rows, axis=1, keepdims=True) + norm_eps)
    return rows * scale, scale


def allowed_block(label_col, label_row, begin, size):
    keys = begin + size
    shape = (size, keys)
    row = begin + lax.broadcasted_iota(jnp.int32, shape, 0)
    col = lax.broadcasted_iota(jnp.int32, shape, 1)
    return (label_col[begin:keys, :] == label_row[:, :keys]) & (col <= row)


def forward_kernel(
    x_ref, gain_ref, wqkv_ref, wout_ref, cos_ref, sin_ref, lcol_ref, lrow_ref, core_ref,
    q_ref, k_ref, v_ref, att_ref, lse_ref, mid_ref, core_out_ref, n1_ref,
):
    rows = x_ref.shape[0]
    core_out_ref[0] = core_ref[0]

    @pl.when(pl.program_id(0) == 0)
    def _():
        x = x_ref[...].astype(F32)
        unit, _ = unit_and_scale(x)
        n1_ref[...] = (unit * gain_ref[...].astype(F32)).astype(BF16)
        mid_ref[...] = x

    proj = dot(n1_ref[...], wqkv_ref[0])
    cos, sin = cos_ref[...], sin_ref[...]
    for head in range(GROUP + 1):
        part = proj[:, head * HEAD_DIM : (head + 1) * HEAD_DIM]
        turned = part * cos + swap_halves(part) * sin
        if head < GROUP:
            q_ref[0, head] = (turned * (HEAD_DIM ** -0.5)).astype(BF16)
        else:
            k_ref[0] = turned.astype(BF16)
    v_ref[0] = proj[:, (GROUP + 1) * HEAD_DIM :].astype(BF16)
    for begin in range(0, rows, ATT_BLOCK):
        stop = begin + ATT_BLOCK
        allowed = allowed_block(lcol_ref, lrow_ref, begin, ATT_BLOCK)
        keys, values = k_ref[0, :stop, :], v_ref[0, :stop, :]
        for head in range(GROUP):
            scores = dot(q_ref[0, head, begin:stop, :], keys, 1, 1)
            scores = jnp.where(allowed, scores, masked_score)
            top = jnp.max(scores, axis=1, keepdims=True)
            weights = jnp.exp(scores - top)
            total = jnp.sum(weights, axis=1, keepdims=True)
            low = (weights * (1.0 / total)).astype(BF16)
            mixed = dot(low, values)
            att_ref[0, begin:stop, head * HEAD_DIM : (head + 1) * HEAD_DIM] = mixed.astype(BF16)
            lse_ref[0, begin:stop, head : head + 1] = top + jnp.log(total)
    mid_ref[...] += dot(att_ref[0], wout_ref[...])


def mlp_kernel(
    mid_ref, cot_ref, live_ref, gain_ref, wg_ref, wu_ref, wd_ref, att_ref,
    out_ref, gm_ref, ga_ref, gb_ref, gain_grad_ref,
    n2_ref, low_ref, acc_ref, gn_ref,
):
    step = pl.program_id(0)

    @pl.when(step == 0)
    def _():
        unit, _ = unit_and_scale(mid_ref[...])
        n2_ref[...] = (unit * gain_ref[...].astype(F32)).astype(BF16)
        low_ref[...] = jnp.where(live_ref[...] > 0, cot_ref[...].astype(F32), 0.0).astype(BF16)
        acc_ref[...] = mid_ref[...]
        gn_ref[...] = jnp.zeros_like(gn_ref)

    n2, low = n2_ref[...], low_ref[...]
    gate = dot(n2, wg_ref[...])
    up = dot(n2, wu_ref[...])
    hidden_grad = dot(low, wd_ref[...], 1, 1)
    sig = jax.nn.sigmoid(gate)
    silu = gate * sig
    hidden = (silu * up).astype(BF16)
    up_grad = (hidden_grad * silu).astype(BF16)
    gate_grad = (hidden_grad * up * sig * (1.0 + gate * (1.0 - sig))).astype(BF16)
    acc_ref[...] += dot(hidden, wd_ref[...])
    gn_ref[...] += dot(gate_grad, wg_ref[...], 1, 1) + dot(up_grad, wu_ref[...], 1, 1)
    rows, lanes = ga_ref.shape[2] // 2, ga_ref.shape[3]
    gate_w = dot(n2, gate_grad, 0, 0).astype(BF16)
    up_w = dot(n2, up_grad, 0, 0).astype(BF16)
    for part in range(2):
        for shard in range(2):
            at = (slice(shard * rows, (shard + 1) * rows), slice(part * lanes, (part + 1) * lanes))
            ga_ref[2 * step + part, shard, :rows, :] = gate_w[at]
            ga_ref[2 * step + part, shard, rows:, :] = up_w[at]
    down_w = dot(hidden, low, 0, 0).astype(BF16)
    size = down_w.shape[0] // 4
    for part in range(4):
        block = down_w[part * size : (part + 1) * size]
        gb_ref[part, step, :size, :] = block[:, :lanes]
        gb_ref[part, step, size : size + size // 2, : lanes // 2] = block[: size // 2, lanes:]
        gb_ref[part, step, size : size + size // 2, lanes // 2 :] = block[size // 2 :, lanes:]

    @pl.when(step == pl.num_programs(0) - 1)
    def _():
        live = live_ref[...] > 0
        out_ref[...] = jnp.where(live, acc_ref[...], 0.0).astype(BF16)
        unit, scale = unit_and_scale(mid_ref[...])
        grad = gn_ref[...]
        gain_grad_ref[...] = jnp.sum(grad * unit, axis=0, keepdims=True)
        scaled = grad * gain_ref[...].astype(F32)
        gm = low_ref[...].astype(F32) + scale * (
            scaled - unit * jnp.mean(scaled * unit, axis=1, keepdims=True)
        )
        gm_ref[...] = gm
        gm_low = gm.astype(BF16)
        grads = [dot(att_ref[group], gm_low, 0, 0) for group in range(KV_HEADS)]
        grads = jnp.concatenate(grads, axis=0)
        piece = grads.shape[0] // 8
        base = size + size // 2
        extra = jnp.zeros((8, grads.shape[1]), F32)
        side = jnp.zeros((piece + 8, 2 * lanes - grads.shape[1]), F32)
        for shard in range(2):
            for part in range(4):
                at = (shard * 4 + part) * piece
                block = jnp.concatenate([grads[at : at + piece], extra], axis=0)
                wide = jnp.concatenate([block[:, lanes:], side], axis=1)
                gb_ref[part, shard, base : base + piece + 8, :] = block[:, :lanes].astype(BF16)
                gb_ref[part, shard, base + piece + 8 :, :] = wide.astype(BF16)


def backward_kernel(
    first, last, x_ref, gain_ref, gm_ref, q_ref, k_ref, v_ref, lse_ref, wqkv_ref, wout_ref,
    cos_ref, sin_ref, lcol_ref, lrow_ref, gain_two_ref, gn_in_ref, after_a_ref, after_b_ref,
    xg_ref, gw_ref,
    n1_ref, low_ref, gn_ref, cat_ref, dk_ref, dv_ref,
):
    rows = x_ref.shape[0]
    unit, scale = unit_and_scale(x_ref[...].astype(F32))
    n1_ref[...] = (unit * gain_ref[...].astype(F32)).astype(BF16)
    low_ref[...] = gm_ref[...].astype(BF16)
    dk_ref[...] = jnp.zeros_like(dk_ref)
    dv_ref[...] = jnp.zeros_like(dv_ref)
    att_grad = dot(low_ref[...], wout_ref[...], 1, 1).astype(BF16)
    for begin in range(0, rows, ATT_BLOCK):
        stop = begin + ATT_BLOCK
        allowed = allowed_block(lcol_ref, lrow_ref, begin, ATT_BLOCK)
        keys, values = k_ref[0, :stop, :], v_ref[0, :stop, :]
        cos, sin = cos_ref[begin:stop, :], sin_ref[begin:stop, :]
        for head in range(GROUP):
            queries = q_ref[0, head, begin:stop, :]
            grads = att_grad[begin:stop, head * HEAD_DIM : (head + 1) * HEAD_DIM]
            scores = jnp.where(allowed, dot(queries, keys, 1, 1), masked_score)
            weights = jnp.exp(scores - lse_ref[0, begin:stop, head : head + 1])
            weight_grad = dot(grads, values, 1, 1)
            centre = jnp.sum(weights * weight_grad, axis=1, keepdims=True)
            score_grad = (weights * (weight_grad - centre)).astype(BF16)
            dk_ref[:stop, :] += dot(score_grad, queries, 0, 0)
            dv_ref[:stop, :] += dot(weights.astype(BF16), grads, 0, 0)
            dq = dot(score_grad, keys) * (HEAD_DIM ** -0.5)
            cat_ref[begin:stop, head * HEAD_DIM : (head + 1) * HEAD_DIM] = (
                dq * cos - swap_halves(dq) * sin
            ).astype(BF16)
    dk = dk_ref[...]
    cat_ref[:, GROUP * HEAD_DIM : (GROUP + 1) * HEAD_DIM] = (
        dk * cos_ref[...] - swap_halves(dk) * sin_ref[...]
    ).astype(BF16)
    cat_ref[:, (GROUP + 1) * HEAD_DIM :] = dv_ref[...].astype(BF16)
    gn_ref[...] = dot(cat_ref[...], wqkv_ref[0], 1, 1)
    if not first:
        gn_ref[...] += gn_in_ref[...]
    grad_w = dot(n1_ref[...], cat_ref[...], 0, 0)
    piece = grad_w.shape[0] // 8
    half = piece * 4
    for shard in range(2):
        tail = jnp.zeros((8, grad_w.shape[1]), F32)
        if last:
            grad = gn_ref[...]
            unit, scale = unit_and_scale(x_ref[...].astype(F32))
            cut = slice(shard * half, (shard + 1) * half)
            gain_sum = jnp.sum(grad * unit, axis=0, keepdims=True)
            tail = jnp.concatenate(
                [gain_sum[:, cut], gain_two_ref[:, cut], jnp.zeros((6, half), F32)], axis=0
            )
            tail = jnp.concatenate([tail, jnp.zeros((8, grad_w.shape[1] - half), F32)], axis=1)
        for part in range(4):
            at = (shard * 4 + part) * piece
            block = jnp.concatenate([grad_w[at : at + piece], tail], axis=0)
            gw_ref[part, shard] = block.astype(BF16)
    if last:
        unit, scale = unit_and_scale(x_ref[...].astype(F32))
        scaled = gn_ref[...] * gain_ref[...].astype(F32)
        xg_ref[...] = (
            gm_ref[...]
            + scale * (scaled - unit * jnp.mean(scaled * unit, axis=1, keepdims=True))
        ).astype(BF16)
    else:
        xg_ref[...] = gn_ref[...]


def assemble_kernel(shard_ref, q_ref, k_ref, v_ref, o_ref, far_ref, qkv_ref, out_ref, core_ref):
    rows = q_ref.shape[0]
    shard = shard_ref[0]
    core_ref[0] = shard_ref[1]
    starts = (0, q_ref.shape[1], q_ref.shape[1] + k_ref.shape[1])
    starts = starts + (starts[2] + v_ref.shape[1],)

    def put(at, parts, out):
        where = slice(at * rows, (at + 1) * rows)
        out_ref[where, :] = out
        for group in range(KV_HEADS):
            begin = 0
            for part, size in zip(parts, (GROUP * HEAD_DIM, HEAD_DIM, HEAD_DIM)):
                qkv_ref[group, where, begin : begin + size] = part[
                    :, group * size : (group + 1) * size
                ]
                begin += size

    for near in range(2):

        @pl.when(shard == near)
        def _():
            put(near, (q_ref[...], k_ref[...], v_ref[...]), o_ref[...])
            far = far_ref[...]
            pieces = tuple(far[:, starts[i] : starts[i + 1]] for i in range(3))
            put(1 - near, pieces, far[:, starts[3] :])


def whole(shape):
    return pl.BlockSpec(shape, lambda i: (0,) * len(shape))


def lead(shape):
    return pl.BlockSpec(shape, lambda i: (i,) + (0,) * (len(shape) - 1))


def params(**more):
    return pltpu.CompilerParams(vmem_limit_bytes=60 * 1024 * 1024, **more)


def take(array, index, axis=0):
    return lax.dynamic_index_in_dim(array, index, axis, keepdims=False)


def swap(array, axis, size, bit):
    return lax.ppermute(array, axis, [(i, i ^ bit) for i in range(size)])


def halve(array, axis, size, bit, mine):
    sent = swap(take(array, 1 - mine), axis, size, bit)
    return (take(array, mine).astype(F32) + sent.astype(F32)).astype(BF16)


def both(array, other, mine):
    return jnp.where(mine == 0, jnp.stack([array, other]), jnp.stack([other, array]))


def reduce_steps(array, core, x, shard, n_rep, shard_first):
    array = halve(array, "rep", n_rep, 1, core)
    yield array
    if shard_first:
        array = halve(jnp.swapaxes(array, 0, 1), "shard", 2, 1, shard)
        yield array
        array = halve(array, "rep", n_rep, 2, x)
    else:
        array = halve(array, "rep", n_rep, 2, x)
        yield array
        array = halve(array, "shard", 2, 1, shard)
    yield array
    bit = 4
    while bit < n_rep:
        array = (array.astype(F32) + swap(array, "rep", n_rep, bit).astype(F32)).astype(BF16)
        bit *= 2
    array = both(array, swap(array, "rep", n_rep, 2), x)
    array = both(array, swap(array, "rep", n_rep, 1), core)
    yield array.reshape((4,) + array.shape[2:])


def fetch_half(first, second, core):
    return swap(jnp.where(core == 0, first, second), "shard", 2, 1)


def exchange_halves(first, second, got, core, shard, n_rep):
    got = jnp.where(core < 2, got, jnp.zeros_like(got))
    other = swap(got, "rep", n_rep, 1)
    far_first = jnp.where(core == 0, got, other)
    far_second = jnp.where(core == 0, other, got)

    def join(near, far):
        return both(near, far, shard).reshape((-1,) + near.shape[1:])

    return join(first, far_first), join(second, far_second)


def local(
    n_rep, n_shard, layer_input, seq_lengths, out_cotangent, attn_gain, w_query, w_key, w_value,
    w_out, mlp_gain, w_gate, w_up, w_down,
):
    rows, width = layer_input.shape
    ff = w_gate.shape[1]
    group_width = GROUP * HEAD_DIM
    packed_width = group_width + 2 * HEAD_DIM
    quick = n_shard == 2 and n_rep >= 4 and n_rep & (n_rep - 1) == 0
    rep, shard = lax.axis_index("rep"), lax.axis_index("shard")
    core, x_bit = rep % 2, (rep // 2) % 2

    own_rows = w_query.shape[0]
    if quick:
        pack = jnp.concatenate([w_query, w_key, w_value, w_out], axis=1)
        far = swap(pack, "shard", 2, 1)
        gains = jnp.stack([attn_gain, mlp_gain])
        far_gains = swap(gains, "shard", 2, 1)
        gains = both(gains, far_gains, shard).swapaxes(0, 1).reshape(2, width)
        gain_one, gain_two = gains[:1], gains[1:]
        qkv_full, out_full, late_core = pl.pallas_call(
            assemble_kernel,
            in_specs=[pl.BlockSpec(memory_space=pltpu.SMEM)]
            + [pl.BlockSpec(memory_space=pltpu.VMEM)] * 5,
            out_specs=[pl.BlockSpec(memory_space=pltpu.VMEM)] * 2
            + [pl.BlockSpec(memory_space=pltpu.SMEM)],
            out_shape=[
                jax.ShapeDtypeStruct((KV_HEADS, width, packed_width), BF16),
                jax.ShapeDtypeStruct((width, width), BF16),
                jax.ShapeDtypeStruct((1,), jnp.int32),
            ],
            compiler_params=params(),
            name="assemble",
        )(jnp.stack([shard, core]).astype(jnp.int32), w_query, w_key, w_value, w_out, far)
        late = late_core[0]
        down_half = w_down.shape[0] // 2
        got_wide = fetch_half(w_gate, w_up, late)
        got_down = fetch_half(w_down[:down_half], w_down[down_half:], late)
    else:
        late_core = core.astype(jnp.int32)[None]
        gather = functools.partial(lax.all_gather, axis_name="shard", axis=0, tiled=True)
        qkv = jnp.concatenate(
            [
                w_query.reshape(own_rows, KV_HEADS, group_width),
                w_key.reshape(own_rows, KV_HEADS, HEAD_DIM),
                w_value.reshape(own_rows, KV_HEADS, HEAD_DIM),
            ],
            axis=2,
        ).reshape(own_rows, -1)
        qkv_full, out_full = gather(qkv), gather(w_out)
        qkv_full = qkv_full.reshape(width, KV_HEADS, packed_width).swapaxes(0, 1)
        gate_full, up_full, down_full = gather(w_gate), gather(w_up), gather(w_down)
        gain_one, gain_two = gather(attn_gain)[None], gather(mlp_gain)[None]

    labels, live_rows, offsets = layout(seq_lengths, rows)
    cosine, sine = rotary_tables(offsets)
    cos_full = jnp.concatenate([cosine, cosine], axis=1)
    sin_full = jnp.concatenate([-sine, sine], axis=1)
    label_col, label_row = labels[:, None], labels[None, :]
    live = live_rows.astype(F32)[:, None]

    shape = jax.ShapeDtypeStruct
    head_block = lead((1, GROUP, rows, HEAD_DIM))
    kv_block = lead((1, rows, HEAD_DIM))
    lse_block = lead((1, rows, GROUP))
    qkv_block = lead((1, width, packed_width))
    out_block = lead((group_width, width))
    tables = [whole((rows, HEAD_DIM))] * 2 + [whole((rows, 1)), whole((1, rows))]
    row_block, gain_block = whole((rows, width)), whole((1, width))
    queries, keys, values, attended, lse, middle, later_core = pl.pallas_call(
        forward_kernel,
        grid=(KV_HEADS,),
        in_specs=[row_block, gain_block, qkv_block, out_block] + tables
        + [pl.BlockSpec(memory_space=pltpu.SMEM)],
        out_specs=[
            head_block, kv_block, kv_block, lead((1, rows, group_width)), lse_block, row_block,
            pl.BlockSpec(memory_space=pltpu.SMEM),
        ],
        out_shape=[
            shape((KV_HEADS, GROUP, rows, HEAD_DIM), BF16),
            shape((KV_HEADS, rows, HEAD_DIM), BF16),
            shape((KV_HEADS, rows, HEAD_DIM), BF16),
            shape((KV_HEADS, rows, group_width), BF16),
            shape((KV_HEADS, rows, GROUP), F32),
            shape((rows, width), F32),
            shape((1,), jnp.int32),
        ],
        scratch_shapes=[pltpu.VMEM((rows, width), BF16)],
        compiler_params=params(),
        cost_estimate=pl.CostEstimate(
            flops=30_000_000_000, bytes_accessed=20_000_000, transcendentals=6_000_000
        ),
        name="attention_forward",
    )(layer_input, gain_one, qkv_full, out_full, cos_full, sin_full, label_col, label_row, late_core)

    if quick:
        later = later_core[0]
        gate_full, up_full = exchange_halves(w_gate, w_up, got_wide, later, shard, n_rep)
        top, low = exchange_halves(
            w_down[:down_half], w_down[down_half:], got_down, later, shard, n_rep
        )
        down_full = jnp.concatenate(
            [top.reshape(2, down_half, width), low.reshape(2, down_half, width)], axis=1
        ).reshape(-1, width)

    steps, parts = 2, 4
    chunk, per_step = ff // steps, parts // steps
    lanes = ff // parts
    piece, half = width // 8, width // 2
    b_rows = ff // 8 + ff // 16 + 2 * (piece + 8)
    layer_output, gm, g_a, g_b, g_gain = pl.pallas_call(
        mlp_kernel,
        grid=(steps,),
        in_specs=[
            row_block, row_block, whole((rows, 1)), gain_block,
            pl.BlockSpec((width, chunk), lambda i: (0, i)),
            pl.BlockSpec((width, chunk), lambda i: (0, i)),
            lead((chunk, width)),
            whole((KV_HEADS, rows, group_width)),
        ],
        out_specs=[
            row_block, row_block,
            whole((parts, 2, width, lanes)),
            whole((parts, 2, b_rows, lanes)),
            gain_block,
        ],
        out_shape=[
            shape((rows, width), BF16),
            shape((rows, width), F32),
            shape((parts, 2, width, lanes), BF16),
            shape((parts, 2, b_rows, lanes), BF16),
            shape((1, width), F32),
        ],
        scratch_shapes=[
            pltpu.VMEM((rows, width), BF16),
            pltpu.VMEM((rows, width), BF16),
            pltpu.VMEM((rows, width), F32),
            pltpu.VMEM((rows, width), F32),
        ],
        compiler_params=params(),
        cost_estimate=pl.CostEstimate(
            flops=30_000_000_000, bytes_accessed=20_000_000, transcendentals=2_000_000
        ),
        name="mlp_both",
    )(middle, out_cotangent, live, gain_two, gate_full, up_full, down_full, attended)

    padded = piece + 8
    g_parts = []
    carried = jnp.zeros((8, 128), F32)

    def steps_of(array, shard_first):
        array = array.reshape((2, 2) + array.shape[1:])
        return reduce_steps(array, core, x_bit, shard, n_rep, shard_first)

    if quick:
        steps_a, steps_b = steps_of(g_a, True), steps_of(g_b, False)
    after = (jnp.zeros((8, 128), BF16),) * 2
    for group in range(KV_HEADS):
        first, last = group == 0, group == KV_HEADS - 1

        def at_group(block, group=group):
            return pl.BlockSpec(block, lambda i: (group,) + (0,) * (len(block) - 1))

        carried, g_part = pl.pallas_call(
            functools.partial(backward_kernel, first, last),
            grid=(1,),
            in_specs=[
                row_block, gain_block, row_block,
                at_group((1, GROUP, rows, HEAD_DIM)), at_group((1, rows, HEAD_DIM)),
                at_group((1, rows, HEAD_DIM)), at_group((1, rows, GROUP)),
                at_group((1, width, packed_width)), at_group((group_width, width)),
            ] + tables + [gain_block, whole(carried.shape)]
            + [pl.BlockSpec(memory_space=pl.ANY)] * 2,
            out_specs=[row_block, whole((4, 2, padded, packed_width))],
            out_shape=[
                shape((rows, width), BF16 if last else F32),
                shape((4, 2, padded, packed_width), BF16),
            ],
            scratch_shapes=[
                pltpu.VMEM((rows, width), BF16),
                pltpu.VMEM((rows, width), BF16),
                pltpu.VMEM((rows, width), F32),
                pltpu.VMEM((rows, packed_width), BF16),
                pltpu.VMEM((rows, HEAD_DIM), F32),
                pltpu.VMEM((rows, HEAD_DIM), F32),
            ],
            compiler_params=params(),
            cost_estimate=pl.CostEstimate(
                flops=15_000_000_000, bytes_accessed=12_000_000, transcendentals=2_000_000
            ),
            name="attention_backward",
        )(
            layer_input, gain_one, gm, queries, keys, values, lse, qkv_full, out_full,
            cos_full, sin_full, label_col, label_row, g_gain, carried, *after,
        )
        if quick:
            after = (next(steps_a), next(steps_b))
        g_parts.append(g_part)
    input_grad = carried
    g_qkv = jnp.stack(g_parts, axis=2)

    def columns(array):
        array = jnp.moveaxis(array, 0, -2)
        return array.reshape(-1, ff)

    def unfold(array):
        cut = ff // 8
        left, right = array[..., :cut, :], array[..., cut : cut + cut // 2, :]
        right = jnp.concatenate([right[..., : lanes // 2], right[..., lanes // 2 :]], axis=-2)
        down = jnp.concatenate([left, right], axis=-1)
        at = cut + cut // 2
        left = array[..., at : at + piece, :]
        right = array[..., at + piece + 8 : at + 2 * piece + 8, : width - lanes]
        return down, jnp.concatenate([left, right], axis=-1)

    if quick:
        *_, got = steps_of(g_qkv, True)
        b_own, a_own = next(steps_b), next(steps_a)
        gate_final, up_final = columns(a_own[:, :half]), columns(a_own[:, half:])
        down_own, out_own = unfold(b_own)
        down_final, out_final = down_own.reshape(-1, width), out_own.reshape(-1, width)
        gain_rows = got[0, KV_HEADS - 1, piece : piece + 2, :half]
        gain_one_final, gain_two_final = gain_rows[0], gain_rows[1]
        qkv_grad = got[:, :, :piece].swapaxes(1, 2).reshape(half, KV_HEADS, packed_width)
    else:
        def sums(array):
            owned = lax.psum_scatter(array, "shard", scatter_dimension=0, tiled=True)
            return lax.psum(owned, "rep")

        gate_final, up_final = sums(columns(g_a[:, :, :half])), sums(columns(g_a[:, :, half:]))
        down_all, out_all = unfold(jnp.swapaxes(g_b, 0, 1))
        down_final, out_final = sums(down_all.reshape(ff, width)), sums(out_all.reshape(width, width))
        gain_rows = g_qkv[0, :, KV_HEADS - 1, piece : piece + 2, :half]
        gain_one_final = sums(gain_rows[:, 0].reshape(width))
        gain_two_final = sums(gain_rows[:, 1].reshape(width))
        qkv_grad = g_qkv[:, :, :, :piece].transpose(1, 0, 3, 2, 4)
        qkv_grad = sums(qkv_grad.reshape(width, KV_HEADS, packed_width))
    own = qkv_grad.shape[0]
    query_final = qkv_grad[:, :, :group_width].reshape(own, -1)
    key_final = qkv_grad[:, :, group_width : group_width + HEAD_DIM].reshape(own, -1)
    value_final = qkv_grad[:, :, group_width + HEAD_DIM :].reshape(own, -1)
    finals = (
        gain_one_final, query_final, key_final, value_final, out_final,
        gain_two_final, gate_final, up_final, down_final,
    )
    return (layer_output, input_grad) + tuple(final.astype(F32) for final in finals)


def solution(mesh):
    return jax.shard_map(
        functools.partial(local, mesh.shape["rep"], mesh.shape["shard"]),
        mesh=mesh,
        in_specs=(
            P(("rep", "shard"), None),
            P(("rep", "shard")),
            P(("rep", "shard"), None),
            P("shard"),
            P("shard", None),
            P("shard", None),
            P("shard", None),
            P("shard", None),
            P("shard"),
            P("shard", None),
            P("shard", None),
            P("shard", None),
        ),
        out_specs=(
            P(("rep", "shard"), None),
            P(("rep", "shard"), None),
            P("shard"),
            P("shard", None),
            P("shard", None),
            P("shard", None),
            P("shard", None),
            P("shard"),
            P("shard", None),
            P("shard", None),
            P("shard", None),
        ),
        check_vma=False,
    )
```
